32 devices in a mesh: groups: 2 (over y), ctx: 8 (over z, x), tp: 2 (over core).
Axes of the slice: x: 2, y: 2, z: 4, core: 2. Of those that a mesh axis runs over, the one named last changes fastest.
Arguments:
- queries: bfloat16 [2048, 2048], P(('groups', 'ctx'), 'tp'), parts along dimension 0, may hold values from -10 to 10
- keys: bfloat16 [2048, 512], P(('groups', 'ctx'), 'tp'), parts along dimension 0, may hold values from -10 to 10
- values: bfloat16 [2048, 512], P(('groups', 'ctx'), 'tp'), parts along dimension 0, may hold values from -6 to 6
- cotangent: bfloat16 [2048, 2048], P(('groups', 'ctx'), 'tp'), parts along dimension 0, may hold values from -6 to 6
- key_probe: bfloat16 [2048, 512], P(('groups', 'ctx'), 'tp'), parts along dimension 0, may hold values from -6 to 6
- value_probe: bfloat16 [2048, 512], P(('groups', 'ctx'), 'tp'), parts along dimension 0, may hold values from -6 to 6
- segments: int32 [2048], P(('groups', 'ctx')), parts along dimension 0, may hold values from 0 to 1, never falling along the last dimension, each value on 1 to 640 neighbouring positions
Outputs:
- hvp_keys: float32 [2048, 512], P(('groups', 'ctx'), 'tp'), parts along dimension 0
- hvp_values: float32 [2048, 512], P(('groups', 'ctx'), 'tp'), parts along dimension 0
The draws below stay inside these ranges and needn't reach their ends.
There are 2 independent parts, one for each index of `groups`. The reference program is written for one: setup_inputs(seed, part) draws one part's arguments, and reference() takes and returns one part's arrays. A program takes and returns all parts, laid end to end along the dimension named above; each array names one. Nothing has to cross between parts.
Inputs may be any that keep to these rules, and one draw needn't show every extreme that they name: `segments`: document numbers never fall along the tokens; each document holds 1 to 640 tokens.
All inputs are finite; a program needn't handle non-finite values.
Results may differ from the reference program's by a relative error of at most 0.0029.
Values may be sent and summed in bfloat16 or wider, within the bound.
A program may use at most 64 MiB of HBM per device.

```python
import math
import jax
import jax.numpy as jnp
import numpy as np
from jax import lax

QUERY_HEAD_COUNT = 16
KEY_VALUE_HEADS = 4
HEAD_WIDTH = 128
TOK_DEV = 128
SPAN = 5
DOC = 640
TOKEN_COUNT = 1024


def draw_keys(key, part):
    key = jax.random.fold_in(key, 3)
    result_output = jnp.clip(jax.random.normal(key, (TOKEN_COUNT, KEY_VALUE_HEADS * HEAD_WIDTH), jnp.float32), -10.0, 10.0)
    return result_output.astype(jnp.bfloat16)


def draw_queries(key, part):
    key = jax.random.fold_in(key, 5)
    result_output = jnp.clip(jax.random.normal(key, (TOKEN_COUNT, QUERY_HEAD_COUNT * HEAD_WIDTH), jnp.float32), -10.0, 10.0)
    return result_output.astype(jnp.bfloat16)


def steps_of(key, dims, cuts, smallest, top_value):
    def one(position, parts):
        draws = jax.random.uniform(jax.random.fold_in(jax.random.fold_in(key, 6), position), (parts,), jnp.float32, smallest / len(cuts), top_value / len(cuts))
        return jnp.repeat(jnp.exp(draws), dims[position] // parts).reshape((-1,) + (1,) * (len(dims) - position - 1))

    factor_of = one(*cuts[0])
    for cut in cuts[1:]:
        factor_of = factor_of * one(*cut)
    return factor_of


def split_up(number_of, total, bound, skew):
    portions = [(1 << 20) // math.isqrt(grade ** skew) + 1 for grade in range(2, number_of + 1)]
    rest, holding = total - bound - (number_of - 1), [1] * (number_of - 1)
    while rest > 0:
        movable = [i for i in range(number_of - 1) if holding[i] < bound]
        pool, budget = sum([portions[i] for i in movable]), rest
        for i in movable:
            more = min(bound - holding[i], max(1, budget * portions[i] // pool), rest)
            holding[i] = holding[i] + more
            rest = rest - more
    return np.array([bound] + holding)


def uneven(rng, count, total, limit, skew):
    if count == 2:
        one = jax.random.randint(rng, (), max(1, total - limit), min(limit, total - 1) + 1)
        return jnp.stack([one, total - one])
    lengths = jnp.asarray(split_up(count, total, limit, skew), jnp.int32)
    couples = (count - 1) // 2
    giver, sink = lengths[1:1 + 2 * couples:2], lengths[2:2 + 2 * couples:2]
    room = jnp.minimum(giver - 1, limit - sink)
    moved = jax.random.randint(jax.random.fold_in(rng, 1), (couples,), 0, 1 << 20) % (room + 1)
    lengths = lengths.at[1:1 + 2 * couples:2].set(giver - moved).at[2:2 + 2 * couples:2].set(sink + moved)
    return lengths[jax.random.permutation(jax.random.fold_in(rng, 2), count)]


def gaussian(stream_key, dims, deviation, most, cuts=(), kind=jnp.bfloat16):
    result = deviation * jax.random.normal(stream_key, dims, jnp.float32)
    if cuts:
        result = result * steps_of(stream_key, dims, cuts, -0.22, 0.18)
    return jnp.clip(result, -most, most).astype(kind)


def setup_inputs(seed: int = 0, part: int = 0) -> dict:
    key_of = jax.random.split(jax.random.key(seed), 8)
    part_splits = jax.random.split(jax.random.fold_in(key_of[7], part), 8)
    return {
        "queries": draw_queries(jax.random.fold_in(jax.random.fold_in(key_of[7], part), 71), part),
        "keys": draw_keys(jax.random.fold_in(jax.random.fold_in(key_of[7], part), 71), part),
        "values": gaussian(part_splits[2], (TOKEN_COUNT, KEY_VALUE_HEADS * HEAD_WIDTH), 1.0, 6.0, ((0, 8), (1, 2))),
        "cotangent": gaussian(part_splits[3], (TOKEN_COUNT, QUERY_HEAD_COUNT * HEAD_WIDTH), 1.0, 6.0, ((0, 8), (1, 2))),
        "key_probe": gaussian(part_splits[4], (TOKEN_COUNT, KEY_VALUE_HEADS * HEAD_WIDTH), 1.0, 6.0, ((0, 8), (1, 2))),
        "value_probe": gaussian(part_splits[5], (TOKEN_COUNT, KEY_VALUE_HEADS * HEAD_WIDTH), 1.0, 6.0, ((0, 8), (1, 2))),
        "segments": jnp.searchsorted(jnp.cumsum(uneven(part_splits[6], TOKEN_COUNT // DOC + 1, TOKEN_COUNT, DOC, 2)), jnp.arange(TOKEN_COUNT), side="right").astype(jnp.int32),
    }


def attend_block(q_block, c_block, k_block, v_block, dk_block, dv_block, keep_mask):
    score_scale = HEAD_WIDTH ** -0.5
    high = lax.Precision.HIGHEST
    raw_score = score_scale * jnp.einsum('thgd,khd->hgtk', q_block, k_block, precision=high)
    masked = jnp.where(keep_mask, raw_score, -jnp.inf)
    top_score = jnp.max(masked, axis=-1, keepdims=True)
    weights = jnp.exp(masked - top_score)
    probability = weights / jnp.sum(weights, axis=-1, keepdims=True)
    along_value = jnp.einsum('thgd,khd->hgtk', c_block, v_block, precision=high)
    slope = score_scale * jnp.einsum('thgd,khd->hgtk', q_block, dk_block, precision=high)
    along_probe = jnp.einsum('thgd,khd->hgtk', c_block, dv_block, precision=high)
    mean_value = jnp.sum(probability * along_value, axis=-1, keepdims=True)
    mean_slope = jnp.sum(probability * slope, axis=-1, keepdims=True)
    mean_cross = jnp.sum(probability * slope * along_value, axis=-1, keepdims=True)
    mean_probe = jnp.sum(probability * along_probe, axis=-1, keepdims=True)
    shift_mean = mean_cross - mean_slope * mean_value + mean_probe
    tangent_prob = probability * (slope - mean_slope)
    tangent_low = tangent_prob.astype(jnp.bfloat16)
    combined = (tangent_prob * (along_value - mean_value) + probability * (along_probe - shift_mean)).astype(jnp.bfloat16)
    value_term = jnp.einsum('hgtk,thgd->khd', tangent_low.astype(jnp.float32), c_block, precision=high)
    key_term = score_scale * jnp.einsum('hgtk,thgd->khd', combined.astype(jnp.float32), q_block, precision=high)
    return key_term, value_term


def reference(queries, keys, values, cotangent, key_probe, value_probe, segments):
    total_rows = queries.shape[0]
    kv_width = keys.shape[1]
    kv_heads = kv_width // HEAD_WIDTH
    group_size = queries.shape[1] // kv_width
    reach = SPAN * TOK_DEV
    window = reach + TOK_DEV

    def padded(array):
        return jnp.concatenate([jnp.zeros((reach, kv_width), array.dtype), array], axis=0)

    key_pad = padded(keys)
    value_pad = padded(values)
    dk_pad = padded(key_probe)
    dv_pad = padded(value_probe)
    label_pad = jnp.concatenate([jnp.full((reach,), -1, jnp.int32), segments.astype(jnp.int32)])

    def one_block(carry, block_index):
        start = (block_index * TOK_DEV).astype(jnp.int32)
        q_block = lax.dynamic_slice_in_dim(queries, start, TOK_DEV, 0).astype(jnp.float32).reshape(TOK_DEV, kv_heads, group_size, HEAD_WIDTH)
        c_block = lax.dynamic_slice_in_dim(cotangent, start, TOK_DEV, 0).astype(jnp.float32).reshape(TOK_DEV, kv_heads, group_size, HEAD_WIDTH)

        def window_of(array):
            return lax.dynamic_slice_in_dim(array, start, window, 0).astype(jnp.float32).reshape(window, kv_heads, HEAD_WIDTH)

        q_labels = lax.dynamic_slice_in_dim(segments.astype(jnp.int32), start, TOK_DEV, 0)
        k_labels = lax.dynamic_slice_in_dim(label_pad, start, window, 0)
        q_pos = start + jnp.arange(TOK_DEV, dtype=jnp.int32)
        k_pos = start - reach + jnp.arange(window, dtype=jnp.int32)
        keep_mask = (q_labels[:, None] == k_labels[None, :]) & (k_pos[None, :] <= q_pos[:, None])
        key_term, value_term = attend_block(q_block, c_block, window_of(key_pad), window_of(value_pad), window_of(dk_pad), window_of(dv_pad), keep_mask)
        update = jnp.stack([key_term, value_term]).reshape(2, window, kv_width)
        current = lax.dynamic_slice_in_dim(carry, start, window, 1)
        carry = lax.dynamic_update_slice_in_dim(carry, current + update, start, 1)
        return carry, None

    initial = jnp.zeros((2, reach + total_rows, kv_width), jnp.float32)
    final_sums, ignored = lax.scan(one_block, initial, jnp.arange(total_rows // TOK_DEV, dtype=jnp.int32))
    return final_sums[0, reach:], final_sums[1, reach:]
```

```python
import functools

import jax
import jax.numpy as jnp
from jax import lax
from jax.experimental import pallas as pl
from jax.experimental.pallas import tpu as pltpu
from jax.sharding import PartitionSpec as P

HEAD_WIDTH = 128
DOC = 640
LABEL_ROWS = 16
MESH = pl.DeviceIdType.MESH
SCALE = HEAD_WIDTH ** (-0.5)
LOG2E = 1.4426950408889634


def lowest_shard(shard, count, rows):
    total = count * rows
    slack = -(-total // DOC) * DOC - total
    margin = -(-slack // rows)
    per_doc = DOC // rows
    start = (shard // per_doc) * per_doc - margin
    if isinstance(shard, int):
        return max(0, start, shard - per_doc)
    return jnp.maximum(jnp.maximum(start, shard - per_doc), 0)


def kernel(count, reach, q_ref, c_ref, k_ref, v_ref, dk_ref, dv_ref, lab_ref, ok_ref, ov_ref,
           pack, inbox, qs, cs, prod, peaks, outbox, retbox, kv_send, kv_recv, ret_send, ret_recv):
    rows, kv_width = k_ref.shape
    heads = kv_width // HEAD_WIDTH
    group = q_ref.shape[1] // kv_width
    wide = group * rows
    me = lax.axis_index("ctx")
    lowest = functools.partial(lowest_shard, count=count, rows=rows)
    gives = [None] + [(me + d < count) & (lowest(me + d) <= me) for d in range(1, reach + 1)]
    takes = [None] + [me - d >= lowest(me) for d in range(1, reach + 1)]

    barrier = pltpu.get_barrier_semaphore()
    for d in range(1, reach + 1):
        @pl.when(gives[d])
        def _():
            pl.semaphore_signal(barrier, inc=1, device_id={"ctx": me + d}, device_id_type=MESH)

        @pl.when(takes[d])
        def _():
            pl.semaphore_signal(barrier, inc=1, device_id={"ctx": me - d}, device_id_type=MESH)

    pack[0:rows, :] = k_ref[...]
    pack[rows : 2 * rows, :] = dk_ref[...]
    pack[2 * rows : 3 * rows, :] = v_ref[...]
    pack[3 * rows : 4 * rows, :] = dv_ref[...]
    my_labels = lab_ref[...].astype(jnp.float32)
    label_rows = jnp.broadcast_to(my_labels, (LABEL_ROWS, rows)).astype(jnp.bfloat16)
    for h in range(kv_width // rows):
        pack[4 * rows :, h * rows : (h + 1) * rows] = label_rows
    partners = 0
    for d in range(1, reach + 1):
        partners = partners + gives[d].astype(jnp.int32) + takes[d].astype(jnp.int32)
    pl.semaphore_wait(barrier, partners)

    def kv_copy(d):
        return pltpu.make_async_remote_copy(
            src_ref=pack, dst_ref=inbox.at[d - 1], send_sem=kv_send.at[d - 1], recv_sem=kv_recv.at[d - 1],
            device_id={"ctx": me + d}, device_id_type=MESH)

    def ret_copy(d):
        return pltpu.make_async_remote_copy(
            src_ref=outbox.at[d - 1], dst_ref=retbox.at[d - 1], send_sem=ret_send.at[d - 1],
            recv_sem=ret_recv.at[d - 1], device_id={"ctx": me - d}, device_id_type=MESH)

    for d in range(1, reach + 1):
        @pl.when(gives[d])
        def _():
            kv_copy(d).start()

    for h in range(heads):
        for g in range(group):
            at = (h * group + g) * HEAD_WIDTH
            qs[h, g * rows : (g + 1) * rows, :] = q_ref[:, at : at + HEAD_WIDTH]
            cs[h, g * rows : (g + 1) * rows, :] = c_ref[:, at : at + HEAD_WIDTH]

    def absorb(d, block):
        their = jnp.broadcast_to(block[4 * rows : 4 * rows + 8, 0:rows].astype(jnp.float32)[0:1], (rows, rows))
        keep = their.T == my_labels
        if d == 0:
            keys = lax.broadcasted_iota(jnp.int32, (rows, rows), 0)
            asks = lax.broadcasted_iota(jnp.int32, (rows, rows), 1)
            keep = keep & (keys <= asks)
        nt = (((1,), (1,)), ((), ()))
        for h in range(heads):
            cols = slice(h * HEAD_WIDTH, (h + 1) * HEAD_WIDTH)
            prod[d, h, 0 : 2 * rows, :] = lax.dot_general(
                block[0 : 2 * rows, cols], qs[h], nt, preferred_element_type=jnp.float32)
            prod[d, h, 2 * rows : 4 * rows, :] = lax.dot_general(
                block[2 * rows : 4 * rows, cols], cs[h], nt, preferred_element_type=jnp.float32)
            for g in range(group):
                lanes = slice(g * rows, (g + 1) * rows)
                masked = jnp.where(keep, prod[d, h, 0:rows, lanes], -jnp.inf)
                top = jnp.max(masked, axis=0, keepdims=True)
                if d > 0:
                    old = peaks[h, 0:1, lanes]
                    top = jnp.maximum(top, old)
                    factor = jnp.exp2((old - top) * (SCALE * LOG2E))
                weight = jnp.exp2((masked - top) * (SCALE * LOG2E))
                prod[d, h, 0:rows, lanes] = weight
                slope = prod[d, h, rows : 2 * rows, lanes]
                along = prod[d, h, 2 * rows : 3 * rows, lanes]
                probed = prod[d, h, 3 * rows : 4 * rows, lanes]
                leaning = weight * slope
                sums = [weight, weight * along, leaning, leaning * along, weight * probed]
                for s, term in enumerate(sums):
                    term = jnp.sum(term, axis=0, keepdims=True)
                    if d > 0:
                        term = term + peaks[h, s + 1 : s + 2, lanes] * factor
                    peaks[h, s + 1 : s + 2, lanes] = term
                peaks[h, 0:1, lanes] = top
                peaks[h, 8 + d : 9 + d, lanes] = top

    absorb(0, pack)
    for d in range(1, reach + 1):
        @pl.when(takes[d])
        def _():
            kv_copy(d).wait_recv()
            absorb(d, inbox.at[d - 1])

    for h in range(heads):
        inverse = 1.0 / peaks[h, 1:2, :]
        mean_a = peaks[h, 2:3, :] * inverse
        mean_s = peaks[h, 3:4, :] * inverse
        mean_c = peaks[h, 4:5, :] * inverse
        mean_p = peaks[h, 5:6, :] * inverse
        peaks[h, 1:2, :] = inverse
        peaks[h, 2:3, :] = mean_a
        peaks[h, 4:5, :] = SCALE * (mean_c - mean_s * mean_a) + mean_p
        peaks[h, 3:4, :] = mean_s

    def terms(d, put):
        for h in range(heads):
            factor = jnp.exp2((peaks[h, 8 + d : 9 + d, :] - peaks[h, 0:1, :]) * (SCALE * LOG2E)) * peaks[h, 1:2, :]
            combined_parts, tangent_parts = [], []
            for g in range(group):
                lanes = slice(g * rows, (g + 1) * rows)
                probability = prod[d, h, 0:rows, lanes] * factor[:, lanes]
                tangent = probability * ((prod[d, h, rows : 2 * rows, lanes] - peaks[h, 3:4, lanes]) * SCALE)
                combined = (tangent * (prod[d, h, 2 * rows : 3 * rows, lanes] - peaks[h, 2:3, lanes])
                            + probability * (prod[d, h, 3 * rows : 4 * rows, lanes] - peaks[h, 4:5, lanes]))
                tangent_parts.append(tangent.astype(jnp.bfloat16))
                combined_parts.append(combined.astype(jnp.bfloat16))
            put(h, SCALE * jnp.dot(jnp.concatenate(combined_parts, axis=1), qs[h],
                                   preferred_element_type=jnp.float32),
                jnp.dot(jnp.concatenate(tangent_parts, axis=1), cs[h], preferred_element_type=jnp.float32))

    for d in range(reach, 0, -1):
        @pl.when(takes[d])
        def _():
            def put(h, key_term, value_term):
                cols = slice(h * HEAD_WIDTH, (h + 1) * HEAD_WIDTH)
                outbox[d - 1, 0:rows, cols] = key_term.astype(jnp.bfloat16)
                outbox[d - 1, rows : 2 * rows, cols] = value_term.astype(jnp.bfloat16)

            terms(d, put)
            ret_copy(d).start()

    def put_own(h, key_term, value_term):
        cols = slice(h * HEAD_WIDTH, (h + 1) * HEAD_WIDTH)
        ok_ref[:, cols] = key_term
        ov_ref[:, cols] = value_term

    terms(0, put_own)

    for d in range(1, reach + 1):
        @pl.when(gives[d])
        def _():
            ret_copy(d).wait_recv()
            ok_ref[...] += retbox[d - 1, 0:rows, :].astype(jnp.float32)
            ov_ref[...] += retbox[d - 1, rows : 2 * rows, :].astype(jnp.float32)

    for d in range(1, reach + 1):
        @pl.when(gives[d])
        def _():
            kv_copy(d).wait_send()

        @pl.when(takes[d])
        def _():
            ret_copy(d).wait_send()


def shards(queries, keys, values, cotangent, key_probe, value_probe, segments):
    rows, kv_width = keys.shape
    heads = kv_width // HEAD_WIDTH
    group = queries.shape[1] // kv_width
    count = lax.axis_size("ctx")
    reach = max(i - lowest_shard(i, count, rows) for i in range(count))
    packed = 4 * rows + LABEL_ROWS
    vmem = pl.BlockSpec(memory_space=pltpu.VMEM)
    shape = jax.ShapeDtypeStruct((rows, kv_width), jnp.float32)
    return pl.pallas_call(
        functools.partial(kernel, count, reach),
        out_shape=(shape, shape),
        in_specs=[vmem] * 7,
        out_specs=(vmem, vmem),
        scratch_shapes=[
            pltpu.VMEM((packed, kv_width), jnp.bfloat16),
            pltpu.VMEM((reach, packed, kv_width), jnp.bfloat16),
            pltpu.VMEM((heads, group * rows, HEAD_WIDTH), jnp.bfloat16),
            pltpu.VMEM((heads, group * rows, HEAD_WIDTH), jnp.bfloat16),
            pltpu.VMEM((reach + 1, heads, 4 * rows, group * rows), jnp.float32),
            pltpu.VMEM((heads, 16, group * rows), jnp.float32),
            pltpu.VMEM((reach, 2 * rows, kv_width), jnp.bfloat16),
            pltpu.VMEM((reach, 2 * rows, kv_width), jnp.bfloat16),
            pltpu.SemaphoreType.DMA((reach,)),
            pltpu.SemaphoreType.DMA((reach,)),
            pltpu.SemaphoreType.DMA((reach,)),
            pltpu.SemaphoreType.DMA((reach,)),
        ],
        compiler_params=pltpu.CompilerParams(
            collective_id=0, has_side_effects=True, vmem_limit_bytes=40 * 1024 * 1024),
        cost_estimate=pl.CostEstimate(flops=1_200_000_000, bytes_accessed=2_000_000, transcendentals=800_000),
    )(queries, cotangent, keys, values, key_probe, value_probe, segments.reshape(1, rows))


def solution(mesh):
    return jax.shard_map(
        shards,
        mesh=mesh,
        in_specs=(P(("groups", "ctx"), "tp"),) * 6 + (P(("groups", "ctx")),),
        out_specs=(P(("groups", "ctx"), "tp"), P(("groups", "ctx"), "tp")),
        check_vma=False,
    )
```

```python
import functools

import jax
import jax.numpy as jnp
from jax import lax
from jax.experimental import pallas as pl
from jax.experimental.pallas import tpu as pltpu
from jax.sharding import PartitionSpec as P

HEAD_WIDTH = 128
DOC = 640
LABEL_ROWS = 16
MESH = pl.DeviceIdType.MESH
SCALE = HEAD_WIDTH ** (-0.5)
LOG2E = 1.4426950408889634


def lowest_shard(shard, count, rows):
    total = count * rows
    slack = -(-total // DOC) * DOC - total
    margin = -(-slack // rows)
    per_doc = DOC // rows
    start = (shard // per_doc) * per_doc - margin
    if isinstance(shard, int):
        return max(0, start, shard - per_doc)
    return jnp.maximum(jnp.maximum(start, shard - per_doc), 0)


ROUTES = (
    (0, None, 0, 2), (0, None, 0, 1), (0, None, 2, 4), (0, 0, 2, 3), (0, 1, 1, 3),
    (1, None, 1, 3), (1, None, 3, 2), (1, None, 3, 5), (1, None, 5, 4),
    (2, None, 2, 4), (2, None, 2, 3),
    (3, None, 3, 5), (3, None, 5, 7), (3, None, 5, 4), (3, None, 7, 6),
    (4, None, 4, 6), (4, None, 4, 5), (4, None, 6, 7),
    (5, None, 5, 7), (5, None, 7, 6),
    (6, None, 6, 7),
)


class Edge:
    def __init__(self, h, a, b, holders, gives):
        self.h, self.a, self.b, self.holders, self.gives = h, a, b, holders, gives

    def sends(self, me):
        if self.holders is None:
            return self.gives(me)
        found = me == self.holders[0]
        for other in self.holders[1:]:
            found = found | (me == other)
        return found

    def receives(self, me):
        step = self.b - self.a
        if self.holders is None:
            return (me >= step) & self.gives(me - step)
        found = me == self.holders[0] + step
        for other in self.holders[1:]:
            found = found | (me == other + step)
        return found


def edges_of(count, rows, heads, reach):
    lowest = functools.partial(lowest_shard, count=count, rows=rows)
    reached = {(j, i) for i in range(count) for j in range(lowest(i), i)}
    routed = {(j, t) for j, _, _, t in ROUTES}
    result = []
    if count == 8 and reached <= routed and DOC // rows == 5:
        table = {}
        for owner, part, start, end in ROUTES:
            for h in range(heads):
                if part is None or h % 2 == part:
                    table.setdefault((h, start - owner, end - owner), []).append(start)
        for (h, a, b), holders in table.items():
            result.append(Edge(h, a, b, holders, None))
    else:
        for d in range(1, reach + 1):
            for h in range(heads):
                result.append(Edge(h, 0, d, None, lambda me, d=d: (me + d < count) & (lowest(me + d) <= me)))
    return result


def either(flags):
    found = flags[0]
    for flag in flags[1:]:
        found = found | flag
    return found


def kernel(count, reach, edges, q_ref, c_ref, k_ref, v_ref, dk_ref, dv_ref, lab_ref, ok_ref, ov_ref,
           labels, pack, inbox, qs, cs, prod, peaks, acc, outbox, retbox,
           load_sem, kv_send, kv_recv, ret_send, ret_recv):
    rows, kv_width = k_ref.shape
    heads = kv_width // HEAD_WIDTH
    group = q_ref.shape[1] // kv_width
    me = lax.axis_index("ctx")
    takes = [None] + [me - d >= lowest_shard(me, count, rows) for d in range(1, reach + 1)]
    sends = [e.sends(me) for e in edges]
    receives = [e.receives(me) for e in edges]
    into = {(d, h): [n for n, e in enumerate(edges) if (e.b, e.h) == (d, h)]
            for d in range(1, reach + 1) for h in range(heads)}
    out_of = {(d, h): [n for n, e in enumerate(edges) if (e.a, e.h) == (d, h)]
              for d in range(reach + 1) for h in range(heads)}

    loads = [pltpu.make_async_copy(lab_ref, labels, load_sem.at[0])]
    for h in range(heads):
        cols = slice(h * HEAD_WIDTH, (h + 1) * HEAD_WIDTH)
        for n, ref in enumerate((k_ref, dk_ref, v_ref, dv_ref)):
            loads.append(pltpu.make_async_copy(
                ref.at[:, cols], pack.at[h, n * rows : (n + 1) * rows, :], load_sem.at[len(loads)]))
    first = len(loads)
    for h in range(heads):
        for g in range(group):
            at = (h * group + g) * HEAD_WIDTH
            for ref, to in ((q_ref, qs), (c_ref, cs)):
                loads.append(pltpu.make_async_copy(
                    ref.at[:, at : at + HEAD_WIDTH], to.at[h, g * rows : (g + 1) * rows, :],
                    load_sem.at[len(loads)]))
    for load in loads:
        load.start()

    barrier = pltpu.get_barrier_semaphore()
    partners = 0
    for step in sorted({e.b - e.a for e in edges}):
        up = either([sends[n] for n, e in enumerate(edges) if e.b - e.a == step])
        down = either([receives[n] for n, e in enumerate(edges) if e.b - e.a == step])

        @pl.when(up)
        def _():
            pl.semaphore_signal(barrier, inc=1, device_id={"ctx": me + step}, device_id_type=MESH)

        @pl.when(down)
        def _():
            pl.semaphore_signal(barrier, inc=1, device_id={"ctx": me - step}, device_id_type=MESH)

        partners = partners + up.astype(jnp.int32) + down.astype(jnp.int32)

    for load in loads[:first]:
        load.wait()
    my_labels = labels[...].astype(jnp.float32)
    for h in range(heads):
        pack[h, 4 * rows :, :] = jnp.broadcast_to(my_labels, (LABEL_ROWS, rows)).astype(jnp.bfloat16)
    pl.semaphore_wait(barrier, partners)

    def kv_copy(n):
        e = edges[n]
        return pltpu.make_async_remote_copy(
            src_ref=pack.at[e.h] if e.a == 0 else inbox.at[e.a - 1, e.h], dst_ref=inbox.at[e.b - 1, e.h],
            send_sem=kv_send.at[n], recv_sem=kv_recv.at[e.b - 1, e.h],
            device_id={"ctx": me + (e.b - e.a)}, device_id_type=MESH)

    def ret_copy(n):
        e = edges[n]
        return pltpu.make_async_remote_copy(
            src_ref=outbox.at[e.b - 1, e.h], dst_ref=retbox.at[n], send_sem=ret_send.at[n],
            recv_sem=ret_recv.at[n], device_id={"ctx": me - (e.b - e.a)}, device_id_type=MESH)

    def pass_on(d, h):
        for n in out_of[d, h]:
            @pl.when(sends[n])
            def _():
                kv_copy(n).start()

    for h in range(heads):
        pass_on(0, h)
    for load in loads[first:]:
        load.wait()

    def absorb(d, h, block):
        their = jnp.broadcast_to(block[4 * rows : 4 * rows + 8, :].astype(jnp.float32)[0:1], (rows, rows))
        keep = their.T == my_labels
        if d == 0:
            keys = lax.broadcasted_iota(jnp.int32, (rows, rows), 0)
            asks = lax.broadcasted_iota(jnp.int32, (rows, rows), 1)
            keep = keep & (keys <= asks)
        nt = (((1,), (1,)), ((), ()))
        prod[d, h, 0 : 2 * rows, :] = lax.dot_general(
            block[0 : 2 * rows, :], qs[h], nt, preferred_element_type=jnp.float32)
        prod[d, h, 2 * rows : 4 * rows, :] = lax.dot_general(
            block[2 * rows : 4 * rows, :], cs[h], nt, preferred_element_type=jnp.float32)
        for g in range(group):
            lanes = slice(g * rows, (g + 1) * rows)
            masked = jnp.where(keep, prod[d, h, 0:rows, lanes], -jnp.inf)
            top = jnp.max(masked, axis=0, keepdims=True)
            if d > 0:
                old = peaks[h, 0:1, lanes]
                top = jnp.maximum(top, old)
                factor = jnp.exp2((old - top) * (SCALE * LOG2E))
            weight = jnp.exp2((masked - top) * (SCALE * LOG2E))
            prod[d, h, 0:rows, lanes] = weight
            slope = prod[d, h, rows : 2 * rows, lanes]
            along = prod[d, h, 2 * rows : 3 * rows, lanes]
            probed = prod[d, h, 3 * rows : 4 * rows, lanes]
            leaning = weight * slope
            sums = [weight, weight * along, leaning, leaning * along, weight * probed]
            for s, term in enumerate(sums):
                term = jnp.sum(term, axis=0, keepdims=True)
                if d > 0:
                    term = term + peaks[h, s + 1 : s + 2, lanes] * factor
                peaks[h, s + 1 : s + 2, lanes] = term
            peaks[h, 0:1, lanes] = top
            peaks[h, 8 + d : 9 + d, lanes] = top

    for h in range(heads):
        absorb(0, h, pack.at[h])
    order = [d for d in (2, 1, 4, 3) if d <= reach] + list(range(5, reach + 1))
    for d in order:
        for h in range(heads):
            if into[d, h]:
                @pl.when(either([receives[n] for n in into[d, h]]))
                def _():
                    kv_copy(into[d, h][0]).wait_recv()
                    pass_on(d, h)

                @pl.when(takes[d])
                def _():
                    absorb(d, h, inbox.at[d - 1, h])

    for h in range(heads):
        inverse = 1.0 / peaks[h, 1:2, :]
        mean_a = peaks[h, 2:3, :] * inverse
        mean_s = peaks[h, 3:4, :] * inverse
        mean_c = peaks[h, 4:5, :] * inverse
        mean_p = peaks[h, 5:6, :] * inverse
        peaks[h, 1:2, :] = inverse
        peaks[h, 2:3, :] = mean_a
        peaks[h, 4:5, :] = SCALE * (mean_c - mean_s * mean_a) + mean_p
        peaks[h, 3:4, :] = mean_s

    def terms(d, h):
        factor = jnp.exp2((peaks[h, 8 + d : 9 + d, :] - peaks[h, 0:1, :]) * (SCALE * LOG2E)) * peaks[h, 1:2, :]
        combined_parts, tangent_parts = [], []
        for g in range(group):
            lanes = slice(g * rows, (g + 1) * rows)
            probability = prod[d, h, 0:rows, lanes] * factor[:, lanes]
            tangent = probability * ((prod[d, h, rows : 2 * rows, lanes] - peaks[h, 3:4, lanes]) * SCALE)
            combined = (tangent * (prod[d, h, 2 * rows : 3 * rows, lanes] - peaks[h, 2:3, lanes])
                        + probability * (prod[d, h, 3 * rows : 4 * rows, lanes] - peaks[h, 4:5, lanes]))
            tangent_parts.append(tangent.astype(jnp.bfloat16))
            combined_parts.append(combined.astype(jnp.bfloat16))
        acc[d, h, 0:rows, :] = SCALE * jnp.dot(
            jnp.concatenate(combined_parts, axis=1), qs[h], preferred_element_type=jnp.float32)
        acc[d, h, rows : 2 * rows, :] = jnp.dot(
            jnp.concatenate(tangent_parts, axis=1), cs[h], preferred_element_type=jnp.float32)

    def give_back(d, h):
        outbox[d - 1, h] = acc[d, h].astype(jnp.bfloat16)
        for n in into[d, h]:
            @pl.when(receives[n])
            def _():
                ret_copy(n).start()

    back = [3, 4, 2, 1] if reach == 4 else list(range(reach, 0, -1))
    for d in back:
        for h in range(heads):
            if into[d, h]:
                @pl.when(takes[d])
                def _():
                    terms(d, h)

                passed = either([receives[n] for n in into[d, h]])
                inner = out_of[d, h] and either([sends[n] for n in out_of[d, h]])
                leaf = passed & ~inner if out_of[d, h] else passed

                @pl.when(leaf)
                def _():
                    give_back(d, h)

    for h in range(heads):
        terms(0, h)

    for d in back + [0]:
        for h in range(heads):
            if not out_of[d, h]:
                continue
            if d > 0:
                inner = either([sends[n] for n in out_of[d, h]])

                @pl.when(inner & ~takes[d])
                def _():
                    acc[d, h] = jnp.zeros_like(acc[d, h])

            for n in out_of[d, h]:
                @pl.when(sends[n])
                def _():
                    ret_copy(n).wait_recv()
                    acc[d, h] += retbox[n].astype(jnp.float32)

            if d > 0:
                @pl.when(inner)
                def _():
                    give_back(d, h)

    for h in range(heads):
        cols = slice(h * HEAD_WIDTH, (h + 1) * HEAD_WIDTH)
        ok_ref[:, cols] = acc[0, h, 0:rows, :]
        ov_ref[:, cols] = acc[0, h, rows : 2 * rows, :]

    for n in range(len(edges)):
        @pl.when(sends[n])
        def _():
            kv_copy(n).wait_send()

        @pl.when(receives[n])
        def _():
            ret_copy(n).wait_send()


def shards(queries, keys, values, cotangent, key_probe, value_probe, segments):
    rows, kv_width = keys.shape
    heads = kv_width // HEAD_WIDTH
    group = queries.shape[1] // kv_width
    count = lax.axis_size("ctx")
    reach = max(i - lowest_shard(i, count, rows) for i in range(count))
    edges = edges_of(count, rows, heads, reach)
    packed = 4 * rows + LABEL_ROWS
    vmem = pl.BlockSpec(memory_space=pltpu.VMEM)
    hbm = pl.BlockSpec(memory_space=pltpu.HBM)
    shape = jax.ShapeDtypeStruct((rows, kv_width), jnp.float32)
    return pl.pallas_call(
        functools.partial(kernel, count, reach, edges),
        out_shape=(shape, shape),
        in_specs=[hbm] * 7,
        out_specs=(vmem, vmem),
        scratch_shapes=[
            pltpu.VMEM((1, rows), jnp.int32),
            pltpu.VMEM((heads, packed, HEAD_WIDTH), jnp.bfloat16),
            pltpu.VMEM((reach, heads, packed, HEAD_WIDTH), jnp.bfloat16),
            pltpu.VMEM((heads, group * rows, HEAD_WIDTH), jnp.bfloat16),
            pltpu.VMEM((heads, group * rows, HEAD_WIDTH), jnp.bfloat16),
            pltpu.VMEM((reach + 1, heads, 4 * rows, group * rows), jnp.float32),
            pltpu.VMEM((heads, 16, group * rows), jnp.float32),
            pltpu.VMEM((reach + 1, heads, 2 * rows, HEAD_WIDTH), jnp.float32),
            pltpu.VMEM((reach, heads, 2 * rows, HEAD_WIDTH), jnp.bfloat16),
            pltpu.VMEM((len(edges), 2 * rows, HEAD_WIDTH), jnp.bfloat16),
            pltpu.SemaphoreType.DMA((1 + heads * (4 + 2 * group),)),
            pltpu.SemaphoreType.DMA((len(edges),)),
            pltpu.SemaphoreType.DMA((reach, heads)),
            pltpu.SemaphoreType.DMA((len(edges),)),
            pltpu.SemaphoreType.DMA((len(edges),)),
        ],
        compiler_params=pltpu.CompilerParams(
            collective_id=0, has_side_effects=True, vmem_limit_bytes=40 * 1024 * 1024),
        cost_estimate=pl.CostEstimate(flops=1_200_000_000, bytes_accessed=2_000_000, transcendentals=800_000),
    )(queries, cotangent, keys, values, key_probe, value_probe, segments.reshape(1, rows))


def solution(mesh):
    return jax.shard_map(
        shards,
        mesh=mesh,
        in_specs=(P(("groups", "ctx"), "tp"),) * 6 + (P(("groups", "ctx")),),
        out_specs=(P(("groups", "ctx"), "tp"), P(("groups", "ctx"), "tp")),
        check_vma=False,
    )
```

```python
import functools

import jax
import jax.numpy as jnp
from jax import lax
from jax.experimental import pallas as pl
from jax.experimental.pallas import tpu as pltpu
from jax.sharding import PartitionSpec as P

HEAD_WIDTH = 128
DOC = 640
LABEL_ROWS = 16
MESH = pl.DeviceIdType.MESH
SCALE = HEAD_WIDTH ** (-0.5)
LOG2E = 1.4426950408889634


def lowest_shard(shard, count, rows):
    total = count * rows
    slack = -(-total // DOC) * DOC - total
    margin = -(-slack // rows)
    per_doc = DOC // rows
    start = (shard // per_doc) * per_doc - margin
    if isinstance(shard, int):
        return max(0, start, shard - per_doc)
    return jnp.maximum(jnp.maximum(start, shard - per_doc), 0)


ROUTES = (
    (0, None, 0, 2), (0, None, 0, 1), (0, None, 2, 4), (0, 0, 2, 3), (0, 1, 1, 3),
    (1, None, 1, 3), (1, None, 3, 2), (1, None, 3, 5), (1, None, 5, 4),
    (2, None, 2, 4), (2, None, 2, 3),
    (3, None, 3, 5), (3, None, 5, 4), (3, None, 5, 7), (3, None, 4, 6),
    (4, None, 4, 6), (4, None, 4, 5), (4, None, 6, 7),
    (5, None, 5, 7), (5, None, 7, 6),
    (6, None, 6, 7),
)
RETURNS = tuple(r for r in ROUTES if r != (3, None, 4, 6)) + ((3, None, 7, 6),)


class Edge:
    def __init__(self, h, a, b, holders, gives):
        self.h, self.a, self.b, self.holders, self.gives = h, a, b, holders, gives

    def sends(self, me):
        if self.holders is None:
            return self.gives(me)
        found = me == self.holders[0]
        for other in self.holders[1:]:
            found = found | (me == other)
        return found

    def receives(self, me):
        step = self.b - self.a
        if self.holders is None:
            return (me >= step) & self.gives(me - step)
        found = me == self.holders[0] + step
        for other in self.holders[1:]:
            found = found | (me == other + step)
        return found


def edges_of(routes, count, rows, heads, reach):
    lowest = functools.partial(lowest_shard, count=count, rows=rows)
    reached = {(j, i) for i in range(count) for j in range(lowest(i), i)}
    routed = {(j, t) for j, _, _, t in routes}
    result = []
    if count == 8 and reached <= routed and DOC // rows == 5:
        table = {}
        for owner, part, start, end in routes:
            for h in range(heads):
                if part is None or h % 2 == part:
                    table.setdefault((h, start - owner, end - owner), []).append(start)
        for (h, a, b), holders in table.items():
            result.append(Edge(h, a, b, holders, None))
    else:
        for d in range(1, reach + 1):
            for h in range(heads):
                result.append(Edge(h, 0, d, None, lambda me, d=d: (me + d < count) & (lowest(me + d) <= me)))
    return result


def either(flags):
    found = flags[0]
    for flag in flags[1:]:
        found = found | flag
    return found


def kernel(count, reach, edges, redges, q_ref, c_ref, k_ref, v_ref, dk_ref, dv_ref, lab_ref, ok_ref, ov_ref,
           labels, pack, inbox, qs, cs, prod, peaks, acc, outbox, retbox,
           load_sem, kv_send, kv_recv, ret_send, ret_recv):
    rows, kv_width = k_ref.shape
    heads = kv_width // HEAD_WIDTH
    group = q_ref.shape[1] // kv_width
    me = lax.axis_index("ctx")
    takes = [None] + [me - d >= lowest_shard(me, count, rows) for d in range(1, reach + 1)]
    units = [(d, h) for d in range(reach + 1) for h in range(heads)]
    sends = [e.sends(me) for e in edges]
    receives = [e.receives(me) for e in edges]
    into = {u: [n for n, e in enumerate(edges) if (e.b, e.h) == u] for u in units}
    out_of = {u: [n for n, e in enumerate(edges) if (e.a, e.h) == u] for u in units}
    adds = [e.sends(me) for e in redges]
    yields = [e.receives(me) for e in redges]
    parents = {u: [n for n, e in enumerate(redges) if (e.b, e.h) == u] for u in units}
    children = {u: [n for n, e in enumerate(redges) if (e.a, e.h) == u] for u in units}

    loads = [pltpu.make_async_copy(lab_ref, labels, load_sem.at[0])]
    for h in range(heads):
        cols = slice(h * HEAD_WIDTH, (h + 1) * HEAD_WIDTH)
        for n, ref in enumerate((k_ref, dk_ref, v_ref, dv_ref)):
            loads.append(pltpu.make_async_copy(
                ref.at[:, cols], pack.at[h, LABEL_ROWS + n * rows : LABEL_ROWS + (n + 1) * rows, :], load_sem.at[len(loads)]))
    first = len(loads)
    for h in range(heads):
        for g in range(group):
            at = (h * group + g) * HEAD_WIDTH
            for ref, to in ((q_ref, qs), (c_ref, cs)):
                loads.append(pltpu.make_async_copy(
                    ref.at[:, at : at + HEAD_WIDTH], to.at[h, g * rows : (g + 1) * rows, :],
                    load_sem.at[len(loads)]))
    for load in loads:
        load.start()

    barrier = pltpu.get_barrier_semaphore()
    partners = 0
    both = [(e, x, y) for e, x, y in zip(edges + redges, sends + adds, receives + yields)]
    forth = [(e.b - e.a, x) for e, x, _ in both] + [(e.a - e.b, y) for e, _, y in both]
    for step in sorted({step for step, _ in forth}):
        up = either([flag for other, flag in forth if other == step])

        @pl.when(up)
        def _():
            pl.semaphore_signal(barrier, inc=1, device_id={"ctx": me + step}, device_id_type=MESH)

        partners = partners + up.astype(jnp.int32)

    for load in loads[:first]:
        load.wait()
    my_labels = labels[...].astype(jnp.float32)
    for h in range(heads):
        pack[h, 0:LABEL_ROWS, :] = jnp.broadcast_to(my_labels, (LABEL_ROWS, rows)).astype(jnp.bfloat16)
    pl.semaphore_wait(barrier, partners)

    middle = LABEL_ROWS + 2 * rows
    cuts = (slice(0, middle), slice(middle, middle + 2 * rows))

    def kv_copy(n, c):
        e = edges[n]
        block = pack.at[e.h] if e.a == 0 else inbox.at[e.a - 1, e.h]
        return pltpu.make_async_remote_copy(
            src_ref=block.at[cuts[c]], dst_ref=inbox.at[e.b - 1, e.h, cuts[c]],
            send_sem=kv_send.at[n, c], recv_sem=kv_recv.at[e.b - 1, e.h, c],
            device_id={"ctx": me + (e.b - e.a)}, device_id_type=MESH)

    def ret_copy(n):
        e = redges[n]
        return pltpu.make_async_remote_copy(
            src_ref=outbox.at[e.b - 1, e.h], dst_ref=retbox.at[n], send_sem=ret_send.at[n],
            recv_sem=ret_recv.at[n], device_id={"ctx": me - (e.b - e.a)}, device_id_type=MESH)

    def pass_on(d, h, c):
        for n in out_of[d, h]:
            @pl.when(sends[n])
            def _():
                kv_copy(n, c).start()

    for h in range(heads):
        for c in range(2):
            pass_on(0, h, c)
    for load in loads[first:]:
        load.wait()

    def absorb(d, h, block):
        their = jnp.broadcast_to(block[0:LABEL_ROWS, :].astype(jnp.float32)[0:1], (rows, rows))
        keep = their.T == my_labels
        if d == 0:
            keys = lax.broadcasted_iota(jnp.int32, (rows, rows), 0)
            asks = lax.broadcasted_iota(jnp.int32, (rows, rows), 1)
            keep = keep & (keys <= asks)
        nt = (((1,), (1,)), ((), ()))
        prod[d, h, 0 : 2 * rows, :] = lax.dot_general(
            block[cuts[0].start + LABEL_ROWS : middle, :], qs[h], nt, preferred_element_type=jnp.float32)
        prod[d, h, 2 * rows : 4 * rows, :] = lax.dot_general(
            block[middle : middle + 2 * rows, :], cs[h], nt, preferred_element_type=jnp.float32)
        for g in range(group):
            lanes = slice(g * rows, (g + 1) * rows)
            masked = jnp.where(keep, prod[d, h, 0:rows, lanes], -jnp.inf)
            top = jnp.max(masked, axis=0, keepdims=True)
            if d > 0:
                old = peaks[h, 0:1, lanes]
                top = jnp.maximum(top, old)
                factor = jnp.exp2((old - top) * (SCALE * LOG2E))
            weight = jnp.exp2((masked - top) * (SCALE * LOG2E))
            prod[d, h, 0:rows, lanes] = weight
            slope = prod[d, h, rows : 2 * rows, lanes]
            along = prod[d, h, 2 * rows : 3 * rows, lanes]
            probed = prod[d, h, 3 * rows : 4 * rows, lanes]
            leaning = weight * slope
            sums = [weight, weight * along, leaning, leaning * along, weight * probed]
            for s, term in enumerate(sums):
                term = jnp.sum(term, axis=0, keepdims=True)
                if d > 0:
                    term = term + peaks[h, s + 1 : s + 2, lanes] * factor
                peaks[h, s + 1 : s + 2, lanes] = term
            peaks[h, 0:1, lanes] = top
            peaks[h, 8 + d : 9 + d, lanes] = top

    for h in range(heads):
        absorb(0, h, pack.at[h])
    order = [d for d in (2, 1, 4, 3) if d <= reach] + list(range(5, reach + 1))
    for d in order:
        for h in range(heads):
            if into[d, h]:
                @pl.when(either([receives[n] for n in into[d, h]]))
                def _():
                    for c in range(2):
                        kv_copy(into[d, h][0], c).wait_recv()
                        pass_on(d, h, c)

                @pl.when(takes[d])
                def _():
                    absorb(d, h, inbox.at[d - 1, h])

    for h in range(heads):
        inverse = 1.0 / peaks[h, 1:2, :]
        mean_a = peaks[h, 2:3, :] * inverse
        mean_s = peaks[h, 3:4, :] * inverse
        mean_c = peaks[h, 4:5, :] * inverse
        mean_p = peaks[h, 5:6, :] * inverse
        peaks[h, 1:2, :] = inverse
        peaks[h, 2:3, :] = mean_a
        peaks[h, 4:5, :] = SCALE * (mean_c - mean_s * mean_a) + mean_p
        peaks[h, 3:4, :] = mean_s

    def terms(d, h):
        factor = jnp.exp2((peaks[h, 8 + d : 9 + d, :] - peaks[h, 0:1, :]) * (SCALE * LOG2E)) * peaks[h, 1:2, :]
        combined_parts, tangent_parts = [], []
        for g in range(group):
            lanes = slice(g * rows, (g + 1) * rows)
            probability = prod[d, h, 0:rows, lanes] * factor[:, lanes]
            tangent = probability * ((prod[d, h, rows : 2 * rows, lanes] - peaks[h, 3:4, lanes]) * SCALE)
            combined = (tangent * (prod[d, h, 2 * rows : 3 * rows, lanes] - peaks[h, 2:3, lanes])
                        + probability * (prod[d, h, 3 * rows : 4 * rows, lanes] - peaks[h, 4:5, lanes]))
            tangent_parts.append(tangent.astype(jnp.bfloat16))
            combined_parts.append(combined.astype(jnp.bfloat16))
        acc[d, h, 0:rows, :] = SCALE * jnp.dot(
            jnp.concatenate(combined_parts, axis=1), qs[h], preferred_element_type=jnp.float32)
        acc[d, h, rows : 2 * rows, :] = jnp.dot(
            jnp.concatenate(tangent_parts, axis=1), cs[h], preferred_element_type=jnp.float32)

    def give_back(d, h):
        outbox[d - 1, h] = acc[d, h].astype(jnp.bfloat16)
        for n in parents[d, h]:
            @pl.when(yields[n])
            def _():
                ret_copy(n).start()

    back = [3, 4, 2, 1] if reach == 4 else list(range(reach, 0, -1))
    for d in back:
        for h in range(heads):
            if parents[d, h]:
                @pl.when(takes[d])
                def _():
                    terms(d, h)

                leaf = either([yields[n] for n in parents[d, h]])
                if children[d, h]:
                    leaf = leaf & ~either([adds[n] for n in children[d, h]])

                @pl.when(leaf)
                def _():
                    give_back(d, h)

    for h in range(heads):
        terms(0, h)

    for d in back + [0]:
        for h in range(heads):
            if not children[d, h]:
                continue
            if d > 0:
                inner = either([adds[n] for n in children[d, h]])

                @pl.when(inner & ~takes[d])
                def _():
                    acc[d, h] = jnp.zeros_like(acc[d, h])

            for n in children[d, h]:
                @pl.when(adds[n])
                def _():
                    ret_copy(n).wait_recv()
                    acc[d, h] += retbox[n].astype(jnp.float32)

            if d > 0:
                @pl.when(inner)
                def _():
                    give_back(d, h)

    for h in range(heads):
        cols = slice(h * HEAD_WIDTH, (h + 1) * HEAD_WIDTH)
        ok_ref[:, cols] = acc[0, h, 0:rows, :]
        ov_ref[:, cols] = acc[0, h, rows : 2 * rows, :]

    for n in range(len(edges)):
        @pl.when(sends[n])
        def _():
            for c in range(2):
                kv_copy(n, c).wait_send()

    for n in range(len(redges)):
        @pl.when(yields[n])
        def _():
            ret_copy(n).wait_send()


def shards(queries, keys, values, cotangent, key_probe, value_probe, segments):
    rows, kv_width = keys.shape
    heads = kv_width // HEAD_WIDTH
    group = queries.shape[1] // kv_width
    count = lax.axis_size("ctx")
    reach = max(i - lowest_shard(i, count, rows) for i in range(count))
    edges = edges_of(ROUTES, count, rows, heads, reach)
    redges = edges_of(RETURNS, count, rows, heads, reach)
    packed = 4 * rows + LABEL_ROWS
    vmem = pl.BlockSpec(memory_space=pltpu.VMEM)
    hbm = pl.BlockSpec(memory_space=pltpu.HBM)
    shape = jax.ShapeDtypeStruct((rows, kv_width), jnp.float32)
    return pl.pallas_call(
        functools.partial(kernel, count, reach, edges, redges),
        out_shape=(shape, shape),
        in_specs=[hbm] * 7,
        out_specs=(vmem, vmem),
        scratch_shapes=[
            pltpu.VMEM((1, rows), jnp.int32),
            pltpu.VMEM((heads, packed, HEAD_WIDTH), jnp.bfloat16),
            pltpu.VMEM((reach, heads, packed, HEAD_WIDTH), jnp.bfloat16),
            pltpu.VMEM((heads, group * rows, HEAD_WIDTH), jnp.bfloat16),
            pltpu.VMEM((heads, group * rows, HEAD_WIDTH), jnp.bfloat16),
            pltpu.VMEM((reach + 1, heads, 4 * rows, group * rows), jnp.float32),
            pltpu.VMEM((heads, 16, group * rows), jnp.float32),
            pltpu.VMEM((reach + 1, heads, 2 * rows, HEAD_WIDTH), jnp.float32),
            pltpu.VMEM((reach, heads, 2 * rows, HEAD_WIDTH), jnp.bfloat16),
            pltpu.VMEM((len(redges), 2 * rows, HEAD_WIDTH), jnp.bfloat16),
            pltpu.SemaphoreType.DMA((1 + heads * (4 + 2 * group),)),
            pltpu.SemaphoreType.DMA((len(edges), 2)),
            pltpu.SemaphoreType.DMA((reach, heads, 2)),
            pltpu.SemaphoreType.DMA((len(redges),)),
            pltpu.SemaphoreType.DMA((len(redges),)),
        ],
        compiler_params=pltpu.CompilerParams(
            collective_id=0, has_side_effects=True, vmem_limit_bytes=64 * 1024 * 1024 - 64 * 1024),
        cost_estimate=pl.CostEstimate(flops=1_200_000_000, bytes_accessed=2_000_000, transcendentals=800_000),
    )(queries, cotangent, keys, values, key_probe, value_probe, segments.reshape(1, rows))


def solution(mesh):
    return jax.shard_map(
        shards,
        mesh=mesh,
        in_specs=(P(("groups", "ctx"), "tp"),) * 6 + (P(("groups", "ctx")),),
        out_specs=(P(("groups", "ctx"), "tp"), P(("groups", "ctx"), "tp")),
        check_vma=False,
    )
```

```python
import functools

import jax
import jax.numpy as jnp
from jax import lax
from jax.experimental import pallas as pl
from jax.experimental.pallas import tpu as pltpu
from jax.sharding import PartitionSpec as P

HEAD_WIDTH = 128
DOC = 640
LABEL_ROWS = 16
MESH = pl.DeviceIdType.MESH
SCALE = HEAD_WIDTH ** (-0.5)
LOG2E = 1.4426950408889634


def lowest_shard(shard, count, rows):
    total = count * rows
    slack = -(-total // DOC) * DOC - total
    margin = -(-slack // rows)
    per_doc = DOC // rows
    start = (shard // per_doc) * per_doc - margin
    if isinstance(shard, int):
        return max(0, start, shard - per_doc)
    return jnp.maximum(jnp.maximum(start, shard - per_doc), 0)


ROUTES = (
    (0, None, 0, 2), (0, None, 0, 1), (0, None, 2, 4), (0, 0, 2, 3), (0, 1, 1, 3),
    (1, None, 1, 3), (1, None, 3, 2), (1, None, 3, 5), (1, None, 5, 4),
    (2, None, 2, 4), (2, None, 2, 3),
    (3, None, 3, 5), (3, None, 5, 4), (3, None, 5, 7), (3, None, 4, 6),
    (4, None, 4, 6), (4, None, 4, 5), (4, None, 6, 7),
    (5, None, 5, 7), (5, None, 7, 6),
    (6, None, 6, 7),
)
RETURNS = (
    (0, None, 0, 2), (0, None, 0, 1), (0, None, 0, 4), (0, 0, 2, 3), (0, 1, 1, 3),
    (1, None, 1, 3), (1, None, 3, 2), (1, None, 1, 5), (1, None, 5, 4),
    (2, None, 2, 4), (2, None, 2, 3),
    (3, None, 3, 5), (3, None, 5, 7), (3, None, 5, 4), (3, None, 7, 6),
    (4, None, 4, 6), (4, None, 4, 5), (4, None, 6, 7),
    (5, None, 5, 7), (5, None, 7, 6),
    (6, None, 6, 7),
)


class Edge:
    def __init__(self, h, a, b, holders, gives):
        self.h, self.a, self.b, self.holders, self.gives = h, a, b, holders, gives

    def sends(self, me):
        if self.holders is None:
            return self.gives(me)
        found = me == self.holders[0]
        for other in self.holders[1:]:
            found = found | (me == other)
        return found

    def receives(self, me):
        step = self.b - self.a
        if self.holders is None:
            return (me >= step) & self.gives(me - step)
        found = me == self.holders[0] + step
        for other in self.holders[1:]:
            found = found | (me == other + step)
        return found


def edges_of(routes, count, rows, heads, reach):
    lowest = functools.partial(lowest_shard, count=count, rows=rows)
    reached = {(j, i) for i in range(count) for j in range(lowest(i), i)}
    routed = {(j, t) for j, _, _, t in routes}
    result = []
    if count == 8 and reached <= routed and DOC // rows == 5:
        table = {}
        for owner, part, start, end in routes:
            for h in range(heads):
                if part is None or h % 2 == part:
                    table.setdefault((h, start - owner, end - owner), []).append(start)
        for (h, a, b), holders in table.items():
            result.append(Edge(h, a, b, holders, None))
    else:
        for d in range(1, reach + 1):
            for h in range(heads):
                result.append(Edge(h, 0, d, None, lambda me, d=d: (me + d < count) & (lowest(me + d) <= me)))
    return result


def either(flags):
    found = flags[0]
    for flag in flags[1:]:
        found = found | flag
    return found


def kernel(count, reach, edges, redges, q_ref, c_ref, k_ref, v_ref, dk_ref, dv_ref, lab_ref, out_ref,
           labels, pack, inbox, qs, cs, prod, peaks, acc, outbox, retbox,
           load_sem, kv_send, kv_recv, ret_send, ret_recv):
    rows, kv_width = k_ref.shape
    heads = kv_width // HEAD_WIDTH
    group = q_ref.shape[1] // kv_width
    me = lax.axis_index("ctx")
    takes = [None] + [me - d >= lowest_shard(me, count, rows) for d in range(1, reach + 1)]
    units = [(d, h) for d in range(reach + 1) for h in range(heads)]
    sends = [e.sends(me) for e in edges]
    receives = [e.receives(me) for e in edges]
    into = {u: [n for n, e in enumerate(edges) if (e.b, e.h) == u] for u in units}
    out_of = {u: [n for n, e in enumerate(edges) if (e.a, e.h) == u] for u in units}
    adds = [e.sends(me) for e in redges]
    yields = [e.receives(me) for e in redges]
    parents = {u: [n for n, e in enumerate(redges) if (e.b, e.h) == u] for u in units}
    children = {u: [n for n, e in enumerate(redges) if (e.a, e.h) == u] for u in units}

    loads = [pltpu.make_async_copy(lab_ref, labels, load_sem.at[0])]
    for h in range(heads):
        cols = slice(h * HEAD_WIDTH, (h + 1) * HEAD_WIDTH)
        for n, ref in enumerate((k_ref, dk_ref, v_ref, dv_ref)):
            loads.append(pltpu.make_async_copy(
                ref.at[:, cols], pack.at[h, LABEL_ROWS + n * rows : LABEL_ROWS + (n + 1) * rows, :], load_sem.at[len(loads)]))
    first = len(loads)
    for h in range(heads):
        for g in range(group):
            at = (h * group + g) * HEAD_WIDTH
            for ref, to in ((q_ref, qs), (c_ref, cs)):
                loads.append(pltpu.make_async_copy(
                    ref.at[:, at : at + HEAD_WIDTH], to.at[h, g * rows : (g + 1) * rows, :],
                    load_sem.at[len(loads)]))
    for load in loads:
        load.start()

    barrier = pltpu.get_barrier_semaphore()
    partners = 0
    both = [(e, x, y) for e, x, y in zip(edges + redges, sends + adds, receives + yields)]
    forth = [(e.b - e.a, x) for e, x, _ in both] + [(e.a - e.b, y) for e, _, y in both]
    for step in sorted({step for step, _ in forth}):
        up = either([flag for other, flag in forth if other == step])

        @pl.when(up)
        def _():
            pl.semaphore_signal(barrier, inc=1, device_id={"ctx": me + step}, device_id_type=MESH)

        partners = partners + up.astype(jnp.int32)

    for load in loads[:first]:
        load.wait()
    my_labels = labels[...].astype(jnp.float32)
    for h in range(heads):
        pack[h, 0:LABEL_ROWS, :] = jnp.broadcast_to(my_labels, (LABEL_ROWS, rows)).astype(jnp.bfloat16)
    pl.semaphore_wait(barrier, partners)

    middle = LABEL_ROWS + 2 * rows
    cuts = (slice(0, middle), slice(middle, middle + 2 * rows))

    def kv_copy(n, c):
        e = edges[n]
        block = pack.at[e.h] if e.a == 0 else inbox.at[e.a - 1, e.h]
        return pltpu.make_async_remote_copy(
            src_ref=block.at[cuts[c]], dst_ref=inbox.at[e.b - 1, e.h, cuts[c]],
            send_sem=kv_send.at[n, c], recv_sem=kv_recv.at[e.b - 1, e.h, c],
            device_id={"ctx": me + (e.b - e.a)}, device_id_type=MESH)

    def ret_copy(n):
        e = redges[n]
        return pltpu.make_async_remote_copy(
            src_ref=outbox.at[e.b - 1, e.h], dst_ref=retbox.at[n], send_sem=ret_send.at[n],
            recv_sem=ret_recv.at[n], device_id={"ctx": me - (e.b - e.a)}, device_id_type=MESH)

    def pass_on(d, h, c):
        for n in out_of[d, h]:
            @pl.when(sends[n])
            def _():
                kv_copy(n, c).start()

    for h in range(heads):
        for c in range(2):
            pass_on(0, h, c)
    for load in loads[first:]:
        load.wait()

    def absorb(d, h, block):
        their = jnp.broadcast_to(block[0:LABEL_ROWS, :].astype(jnp.float32)[0:1], (rows, rows))
        keep = their.T == my_labels
        if d == 0:
            keys = lax.broadcasted_iota(jnp.int32, (rows, rows), 0)
            asks = lax.broadcasted_iota(jnp.int32, (rows, rows), 1)
            keep = keep & (keys <= asks)
        nt = (((1,), (1,)), ((), ()))
        prod[d, h, 0 : 2 * rows, :] = lax.dot_general(
            block[cuts[0].start + LABEL_ROWS : middle, :], qs[h], nt, preferred_element_type=jnp.float32)
        prod[d, h, 2 * rows : 4 * rows, :] = lax.dot_general(
            block[middle : middle + 2 * rows, :], cs[h], nt, preferred_element_type=jnp.float32)
        for g in range(group):
            lanes = slice(g * rows, (g + 1) * rows)
            masked = jnp.where(keep, prod[d, h, 0:rows, lanes], -jnp.inf)
            top = jnp.max(masked, axis=0, keepdims=True)
            if d > 0:
                old = peaks[h, 0:1, lanes]
                top = jnp.maximum(top, old)
                factor = jnp.exp2((old - top) * (SCALE * LOG2E))
            weight = jnp.exp2((masked - top) * (SCALE * LOG2E))
            prod[d, h, 0:rows, lanes] = weight
            slope = prod[d, h, rows : 2 * rows, lanes]
            along = prod[d, h, 2 * rows : 3 * rows, lanes]
            probed = prod[d, h, 3 * rows : 4 * rows, lanes]
            leaning = weight * slope
            sums = [weight, weight * along, leaning, leaning * along, weight * probed]
            for s, term in enumerate(sums):
                term = jnp.sum(term, axis=0, keepdims=True)
                if d > 0:
                    term = term + peaks[h, s + 1 : s + 2, lanes] * factor
                peaks[h, s + 1 : s + 2, lanes] = term
            peaks[h, 0:1, lanes] = top
            peaks[h, 8 + d : 9 + d, lanes] = top

    for h in range(heads):
        absorb(0, h, pack.at[h])
    order = [d for d in (2, 1, 4, 3) if d <= reach] + list(range(5, reach + 1))
    for d in order:
        for h in range(heads):
            if into[d, h]:
                @pl.when(either([receives[n] for n in into[d, h]]))
                def _():
                    for c in range(2):
                        kv_copy(into[d, h][0], c).wait_recv()
                        pass_on(d, h, c)

                @pl.when(takes[d])
                def _():
                    absorb(d, h, inbox.at[d - 1, h])

    for h in range(heads):
        inverse = 1.0 / peaks[h, 1:2, :]
        mean_a = peaks[h, 2:3, :] * inverse
        mean_s = peaks[h, 3:4, :] * inverse
        mean_c = peaks[h, 4:5, :] * inverse
        mean_p = peaks[h, 5:6, :] * inverse
        peaks[h, 1:2, :] = inverse
        peaks[h, 2:3, :] = mean_a
        peaks[h, 4:5, :] = SCALE * (mean_c - mean_s * mean_a) + mean_p
        peaks[h, 3:4, :] = mean_s

    def terms(d, h):
        factor = jnp.exp2((peaks[h, 8 + d : 9 + d, :] - peaks[h, 0:1, :]) * (SCALE * LOG2E)) * peaks[h, 1:2, :]
        combined_parts, tangent_parts = [], []
        for g in range(group):
            lanes = slice(g * rows, (g + 1) * rows)
            probability = prod[d, h, 0:rows, lanes] * factor[:, lanes]
            tangent = probability * ((prod[d, h, rows : 2 * rows, lanes] - peaks[h, 3:4, lanes]) * SCALE)
            combined = (tangent * (prod[d, h, 2 * rows : 3 * rows, lanes] - peaks[h, 2:3, lanes])
                        + probability * (prod[d, h, 3 * rows : 4 * rows, lanes] - peaks[h, 4:5, lanes]))
            tangent_parts.append(tangent.astype(jnp.bfloat16))
            combined_parts.append(combined.astype(jnp.bfloat16))
        acc[d, h, 0:rows, :] = SCALE * jnp.dot(
            jnp.concatenate(combined_parts, axis=1), qs[h], preferred_element_type=jnp.float32)
        acc[d, h, rows : 2 * rows, :] = jnp.dot(
            jnp.concatenate(tangent_parts, axis=1), cs[h], preferred_element_type=jnp.float32)

    def give_back(d, h):
        outbox[d - 1, h] = acc[d, h].astype(jnp.bfloat16)
        for n in parents[d, h]:
            @pl.when(yields[n])
            def _():
                ret_copy(n).start()

    back = [3, 4, 2, 1] if reach == 4 else list(range(reach, 0, -1))
    for d in back:
        for h in range(heads):
            if parents[d, h]:
                @pl.when(takes[d])
                def _():
                    terms(d, h)

                leaf = either([yields[n] for n in parents[d, h]])
                if children[d, h]:
                    leaf = leaf & ~either([adds[n] for n in children[d, h]])

                @pl.when(leaf)
                def _():
                    give_back(d, h)

    for h in range(heads):
        terms(0, h)

    for d in back + [0]:
        for h in range(heads):
            if not children[d, h]:
                continue
            if d > 0:
                inner = either([adds[n] for n in children[d, h]])

                @pl.when(inner & ~takes[d])
                def _():
                    acc[d, h] = jnp.zeros_like(acc[d, h])

            for n in children[d, h]:
                @pl.when(adds[n])
                def _():
                    ret_copy(n).wait_recv()
                    acc[d, h] += retbox[n].astype(jnp.float32)

            if d > 0:
                @pl.when(inner)
                def _():
                    give_back(d, h)

    for h in range(heads):
        cols = slice(h * HEAD_WIDTH, (h + 1) * HEAD_WIDTH)
        out_ref[0:rows, cols] = acc[0, h, 0:rows, :]
        out_ref[rows : 2 * rows, cols] = acc[0, h, rows : 2 * rows, :]

    for n in range(len(edges)):
        @pl.when(sends[n])
        def _():
            for c in range(2):
                kv_copy(n, c).wait_send()

    for n in range(len(redges)):
        @pl.when(yields[n])
        def _():
            ret_copy(n).wait_send()


def shards(queries, keys, values, cotangent, key_probe, value_probe, segments):
    rows, kv_width = keys.shape
    heads = kv_width // HEAD_WIDTH
    group = queries.shape[1] // kv_width
    count = lax.axis_size("ctx")
    reach = max(i - lowest_shard(i, count, rows) for i in range(count))
    edges = edges_of(ROUTES, count, rows, heads, reach)
    redges = edges_of(RETURNS, count, rows, heads, reach)
    packed = 4 * rows + LABEL_ROWS
    vmem = pl.BlockSpec(memory_space=pltpu.VMEM)
    hbm = pl.BlockSpec(memory_space=pltpu.HBM)
    shape = jax.ShapeDtypeStruct((2 * rows, kv_width), jnp.float32)
    both = pl.pallas_call(
        functools.partial(kernel, count, reach, edges, redges),
        out_shape=shape,
        in_specs=[hbm] * 7,
        out_specs=vmem,
        scratch_shapes=[
            pltpu.VMEM((1, rows), jnp.int32),
            pltpu.VMEM((heads, packed, HEAD_WIDTH), jnp.bfloat16),
            pltpu.VMEM((reach, heads, packed, HEAD_WIDTH), jnp.bfloat16),
            pltpu.VMEM((heads, group * rows, HEAD_WIDTH), jnp.bfloat16),
            pltpu.VMEM((heads, group * rows, HEAD_WIDTH), jnp.bfloat16),
            pltpu.VMEM((reach + 1, heads, 4 * rows, group * rows), jnp.float32),
            pltpu.VMEM((heads, 16, group * rows), jnp.float32),
            pltpu.VMEM((reach + 1, heads, 2 * rows, HEAD_WIDTH), jnp.float32),
            pltpu.VMEM((reach, heads, 2 * rows, HEAD_WIDTH), jnp.bfloat16),
            pltpu.VMEM((len(redges), 2 * rows, HEAD_WIDTH), jnp.bfloat16),
            pltpu.SemaphoreType.DMA((1 + heads * (4 + 2 * group),)),
            pltpu.SemaphoreType.DMA((len(edges), 2)),
            pltpu.SemaphoreType.DMA((reach, heads, 2)),
            pltpu.SemaphoreType.DMA((len(redges),)),
            pltpu.SemaphoreType.DMA((len(redges),)),
        ],
        compiler_params=pltpu.CompilerParams(
            collective_id=0, has_side_effects=True, vmem_limit_bytes=64 * 1024 * 1024 - 64 * 1024),
        cost_estimate=pl.CostEstimate(flops=1_200_000_000, bytes_accessed=2_000_000, transcendentals=800_000),
    )(queries, cotangent, keys, values, key_probe, value_probe, segments.reshape(1, rows))
    return both[:rows], both[rows:]


def solution(mesh):
    return jax.shard_map(
        shards,
        mesh=mesh,
        in_specs=(P(("groups", "ctx"), "tp"),) * 6 + (P(("groups", "ctx")),),
        out_specs=(P(("groups", "ctx"), "tp"), P(("groups", "ctx"), "tp")),
        check_vma=False,
    )
```
